128 devices in a mesh: row: 8 (over y_hi, z), col: 16 (over y_lo, x, core).
Axes of the slice: x: 4, y: 4 (y_hi: 2, y_lo: 2; y = y_hi * 2 + y_lo), z: 4, core: 2. Of those that a mesh axis runs over, the one named last changes fastest.
Arguments:
- vectors: bfloat16 [65536, 256], P(('row', 'col')), may hold values from -6 to 6
- blocks: bfloat16 [8, 16, 256, 128, 128], P('row', 'col'), may hold values from -0.046875 to 0.046875
- block_rows: int32 [8, 16, 256], P('row', 'col'), may hold values from 0 to 63
- block_cols: int32 [8, 16, 256], P('row', 'col'), may hold values from 0 to 31
- block_count: int32 [8, 16], P('row', 'col'), may hold values from 32 to 256, as said below
- lower_edge: float32 [1], replicated, may hold values from -0.6 to -0.3
- upper_edge: float32 [1], replicated, may hold values from 1 to 2
Outputs:
- filtered: float32 [65536, 256], P(('row', 'col'))
The draws below stay inside these ranges and needn't reach their ends.
Inputs may be any that keep to these rules, and one draw needn't show every extreme that they name: `block_count`: some device has all 256 slots live.
All inputs are finite; a program needn't handle non-finite values.
Results may differ from the reference program's by a relative error of at most 0.008.
Values may be sent and summed in bfloat16 or wider, within the bound.
No kernel may reach another device: no remote copies, remote signals or barrier semaphores. Data moves between devices by JAX's collectives and lax.ppermute only.
A program may use at most 192 MiB of HBM per device.

```python
import jax
import jax.numpy as jnp
from jax import lax

BLOCK = 128
VECS = 256
SEG = 512
BLK_DEV = 256
DEGREE = 2
ORDER = 65536
N_ROW = 8
N_COL = 16


def draw_block_count(key, part):
    key = jax.random.fold_in(key, 7)
    key_counts, key_busy = jax.random.split(key)
    counts = jax.random.randint(key_counts, (N_ROW, N_COL), BLK_DEV // 8, BLK_DEV // 2 + 1)
    busiest = jax.random.randint(key_busy, (), 0, N_ROW * N_COL)
    flattened = jnp.where(jnp.arange(N_ROW * N_COL) == busiest, BLK_DEV, counts.reshape(-1))
    return flattened.reshape(N_ROW, N_COL).astype(jnp.int32)


def touch_ends(entries, own_key, least, largest):
    index_at = [jax.random.randint(jax.random.fold_in(own_key, axis), (), 0, length) for axis, length in enumerate(entries.shape)]
    main_axis = entries.shape.index(max(entries.shape))
    neighbour = index_at[:main_axis] + [(index_at[main_axis] + 1) % entries.shape[main_axis]] + index_at[main_axis + 1:]
    return entries.at[tuple(index_at)].set(least).at[tuple(neighbour)].set(largest)


def level_of(own_key, dims, pieces, smallest, largest):
    def one(dim, parts):
        steps = jax.random.uniform(jax.random.fold_in(jax.random.fold_in(own_key, 6), dim), (parts,), jnp.float32, smallest / len(pieces), largest / len(pieces))
        return jnp.repeat(jnp.exp(steps), dims[dim] // parts).reshape((-1,) + (1,) * (len(dims) - dim - 1))

    loudness = one(*pieces[0])
    for cut in pieces[1:]:
        loudness = loudness * one(*cut)
    return loudness


def bell_draw(stream_key, dims, scale, reach, cuts=(), held_as=jnp.bfloat16):
    array = scale * jax.random.normal(stream_key, dims, jnp.float32)
    if cuts:
        array = array * level_of(stream_key, dims, cuts, -0.22, 0.18)
    return jnp.clip(array, -reach, reach).astype(held_as)


def setup_inputs(seed: int = 0) -> dict:
    arg_keys = jax.random.split(jax.random.key(seed), 8)
    vectors = bell_draw(arg_keys[0], (ORDER, VECS), 1.0, 6.0, ((0, 128),))
    blocks = bell_draw(arg_keys[1], (N_ROW, N_COL, BLK_DEV, BLOCK, BLOCK), (2 * BLK_DEV * BLOCK * BLOCK // SEG) ** -0.5, 0.046875, ((0, 8), (1, 16)))
    block_rows = touch_ends(jax.random.randint(arg_keys[2], (N_ROW, N_COL, BLK_DEV), 0, N_COL * SEG // BLOCK), jax.random.fold_in(arg_keys[2], 1), 0, (N_COL * SEG // BLOCK) - 1).astype(jnp.int32)
    block_cols = touch_ends(jax.random.randint(arg_keys[3], (N_ROW, N_COL, BLK_DEV), 0, N_ROW * SEG // BLOCK), jax.random.fold_in(arg_keys[3], 1), 0, (N_ROW * SEG // BLOCK) - 1).astype(jnp.int32)
    block_count = draw_block_count(jax.random.fold_in(arg_keys[7], 71), 0)
    lower_edge = jnp.clip(jax.random.uniform(arg_keys[5], (1,), jnp.float32, -0.6, -0.3), -0.6, -0.3)
    upper_edge = jnp.clip(jax.random.uniform(arg_keys[6], (1,), jnp.float32, 1.0, 2.0), 1.0, 2.0)
    return {"vectors": vectors, "blocks": blocks, "block_rows": block_rows, "block_cols": block_cols, "block_count": block_count, "lower_edge": lower_edge, "upper_edge": upper_edge}


def applied_product(operand, blocks, block_rows, block_cols, block_count):
    vec_width = operand.shape[1]
    vector_grid = operand.reshape(N_ROW, N_COL, SEG, vec_width)

    def device_step(totals, device):
        row_pos = device // N_COL
        col_pos = device % N_COL
        rows_side = lax.dynamic_index_in_dim(vector_grid, row_pos, 0, keepdims=False).reshape(-1, BLOCK, vec_width)
        cols_side = lax.dynamic_index_in_dim(vector_grid, col_pos, 1, keepdims=False).reshape(-1, BLOCK, vec_width)
        row_blocks = lax.dynamic_index_in_dim(blocks, row_pos, 0, keepdims=False)
        block_tile = lax.dynamic_index_in_dim(row_blocks, col_pos, 0, keepdims=False).astype(jnp.float32)
        rows_here = block_rows[row_pos, col_pos]
        cols_here = block_cols[row_pos, col_pos]
        live_mask = (jnp.arange(BLK_DEV) < block_count[row_pos, col_pos]).astype(jnp.float32)[:, None, None]
        forward = jnp.einsum('gij,gjv->giv', block_tile, cols_side[cols_here].astype(jnp.float32)) * live_mask
        mirror = jnp.einsum('gji,gjv->giv', block_tile, rows_side[rows_here].astype(jnp.float32)) * live_mask
        row_part = jnp.zeros(rows_side.shape, jnp.float32).at[rows_here].add(forward)
        col_part = jnp.zeros(cols_side.shape, jnp.float32).at[cols_here].add(mirror)
        totals = totals.at[row_pos].add(row_part.reshape(N_COL, SEG, vec_width))
        totals = totals.at[:, col_pos].add(col_part.reshape(N_ROW, SEG, vec_width))
        return totals, None

    totals = jnp.zeros((N_ROW, N_COL, SEG, vec_width), jnp.float32)
    totals, unused = lax.scan(device_step, totals, jnp.arange(N_ROW * N_COL, dtype=jnp.int32))
    return totals.reshape(-1, vec_width)


def reference(vectors, blocks, block_rows, block_cols, block_count, lower_edge, upper_edge):
    center = (upper_edge[0] + lower_edge[0]) * 0.5
    half_width = (upper_edge[0] - lower_edge[0]) * 0.5
    current = vectors.astype(jnp.float32)
    previous = jnp.zeros_like(current)
    for degree in range(DEGREE):
        operand = current.astype(jnp.bfloat16)
        applied = applied_product(operand, blocks, block_rows, block_cols, block_count)
        shifted = applied - center * current
        if degree == 0:
            following = shifted / half_width
        else:
            following = 2.0 * shifted / half_width - previous
        previous, current = current, following
    return current
```

```python
import functools

import jax
import jax.numpy as jnp
from jax import lax
from jax.experimental import pallas as pl
from jax.experimental.pallas import tpu as pltpu
from jax.sharding import PartitionSpec as P

DEGREE = 2
UNROLL = 4


def slot_kernel(
    rows_ref, cols_ref, count_ref, blocks_ref, row_side, col_side, row_out, col_out, row_acc, col_acc
):
    group = pl.program_id(0)
    group_size = blocks_ref.shape[0]

    @pl.when(group == 0)
    def _():
        row_acc[...] = jnp.zeros_like(row_acc)
        col_acc[...] = jnp.zeros_like(col_acc)

    first = group * group_size
    live = jnp.clip(count_ref[0] - first, 0, group_size)

    def one_slot(k):
        row = rows_ref[first + k]
        col = cols_ref[first + k]
        block = blocks_ref[k]
        forward = jnp.dot(block, col_side[col], preferred_element_type=jnp.float32)
        mirror = lax.dot_general(
            block, row_side[row], (((0,), (0,)), ((), ())), preferred_element_type=jnp.float32
        )
        return row, col, forward, mirror

    def add(found):
        row, col, forward, mirror = found
        row_acc[row] += forward
        col_acc[col] += mirror

    def step(i, carry):
        found = [one_slot(i * UNROLL + u) for u in range(UNROLL)]
        for f in found:
            add(f)
        return carry

    whole = live // UNROLL
    lax.fori_loop(0, whole, step, 0)

    def rest(k, carry):
        add(one_slot(k))
        return carry

    lax.fori_loop(whole * UNROLL, live, rest, 0)

    @pl.when(group == pl.num_programs(0) - 1)
    def _():
        row_out[...] = row_acc[...].astype(row_out.dtype)
        col_out[...] = col_acc[...].astype(col_out.dtype)


def slot_products(local_blocks, local_rows, local_cols, slot_count, rows_side, cols_side):
    slots, order, _ = local_blocks.shape
    width = rows_side.shape[1]
    row_tiles = rows_side.reshape(-1, order, width)
    col_tiles = cols_side.reshape(-1, order, width)
    group_size = min(32, slots)

    def block_map(g, rows, cols, count):
        last = jnp.maximum((count[0] + group_size - 1) // group_size - 1, 0)
        return (jnp.minimum(g, last), 0, 0)

    def whole(g, rows, cols, count):
        return (0, 0, 0)

    row_part, col_part = pl.pallas_call(
        slot_kernel,
        grid_spec=pltpu.PrefetchScalarGridSpec(
            num_scalar_prefetch=3,
            grid=(slots // group_size,),
            in_specs=[
                pl.BlockSpec((group_size, order, order), block_map),
                pl.BlockSpec(row_tiles.shape, whole, pipeline_mode=pl.Buffered(1)),
                pl.BlockSpec(col_tiles.shape, whole, pipeline_mode=pl.Buffered(1)),
            ],
            out_specs=[
                pl.BlockSpec(row_tiles.shape, whole, pipeline_mode=pl.Buffered(1)),
                pl.BlockSpec(col_tiles.shape, whole, pipeline_mode=pl.Buffered(1)),
            ],
            scratch_shapes=[
                pltpu.VMEM(row_tiles.shape, jnp.float32),
                pltpu.VMEM(col_tiles.shape, jnp.float32),
            ],
        ),
        out_shape=[
            jax.ShapeDtypeStruct(row_tiles.shape, jnp.bfloat16),
            jax.ShapeDtypeStruct(col_tiles.shape, jnp.bfloat16),
        ],
        compiler_params=pltpu.CompilerParams(vmem_limit_bytes=44 * 1024 * 1024),
        cost_estimate=pl.CostEstimate(
            flops=4 * slots * order * order * width, bytes_accessed=20 * 1024 * 1024, transcendentals=0
        ),
    )(local_rows, local_cols, slot_count, local_blocks, row_tiles, col_tiles)
    return row_part.reshape(-1, width), col_part.reshape(-1, width)


def split_sum(part, axis, members):
    pieces = lax.all_to_all(part, axis, 0, 0, tiled=True)
    pieces = pieces.reshape(members, -1, part.shape[1])
    return jnp.sum(pieces.astype(jnp.float32), axis=0)


def per_device(
    vectors, blocks, block_rows, block_cols, block_count, lower_edge, upper_edge, *, row_size, col_size
):
    center = (upper_edge[0] + lower_edge[0]) * 0.5
    half_width = (upper_edge[0] - lower_edge[0]) * 0.5
    local_blocks = blocks[0, 0]
    local_rows = block_rows[0, 0]
    local_cols = block_cols[0, 0]
    slot_count = block_count[0]
    current = vectors.astype(jnp.float32)
    previous = jnp.zeros_like(current)
    for degree in range(DEGREE):
        operand = current.astype(jnp.bfloat16)
        cols_side = lax.all_gather(operand, "row", axis=0, tiled=True)
        rows_side = lax.all_gather(operand, "col", axis=0, tiled=True)
        row_part, col_part = slot_products(
            local_blocks, local_rows, local_cols, slot_count, rows_side, cols_side
        )
        applied = split_sum(row_part, "col", col_size) + split_sum(col_part, "row", row_size)
        shifted = applied - center * current
        if degree == 0:
            following = shifted / half_width
        else:
            following = 2.0 * shifted / half_width - previous
        previous, current = (current, following)
    return current


def solution(mesh):
    sizes = dict(mesh.shape)
    return jax.shard_map(
        functools.partial(per_device, row_size=sizes["row"], col_size=sizes["col"]),
        mesh=mesh,
        in_specs=(
            P(("row", "col"), None),
            P("row", "col", None, None, None),
            P("row", "col", None),
            P("row", "col", None),
            P("row", "col"),
            P(),
            P(),
        ),
        out_specs=P(("row", "col"), None),
        check_vma=False,
    )
```

```python
import functools
import itertools

import jax
import jax.numpy as jnp
from jax import lax
from jax.experimental import pallas as pl
from jax.experimental.pallas import tpu as pltpu
from jax.sharding import PartitionSpec as P

DEGREE = 2
UNROLL = 16
GROUP = 64
BOTH = ("row", "col")


def linear(y_hi, z, y_lo, x, core):
    return (y_hi * 4 + z) * 16 + y_lo * 8 + x * 2 + core


def pairs(move):
    every = itertools.product(range(2), range(4), range(2), range(4), range(2))
    return [(linear(*d), linear(*move(*d))) for d in every]


def ring_first(core):
    return 3 if core else 1


def ring_second(core):
    return 1 if core else 3


TO_CORE = pairs(lambda h, z, l, x, k: (h, z, l, x, k ^ 1))
ROW_MOVES = (
    pairs(lambda h, z, l, x, k: (h, z, l ^ 1, x, k)),
    pairs(lambda h, z, l, x, k: (h, z, l, x ^ ring_first(k), k)),
    pairs(lambda h, z, l, x, k: (h, z, l, x ^ ring_second(k), k)),
)
COL_MOVES = (
    pairs(lambda h, z, l, x, k: (h ^ 1, z, l, x, k)),
    pairs(lambda h, z, l, x, k: (h, z ^ ring_first(k), l, x, k)),
    pairs(lambda h, z, l, x, k: (h, z ^ ring_second(k), l, x, k)),
)


def move(value, table):
    return lax.ppermute(value, BOTH, table)


def slot_kernel(
    row_tile_ref, col_tile_ref, count_ref, own_ref, mate_ref, row_near, row_far, col_near, col_far,
    row_send, row_keep, col_send, col_keep, row_side, col_side, row_acc, col_acc, sems,
):
    step_index = pl.program_id(0)
    groups = pl.num_programs(0) // 2
    size = own_ref.shape[0]
    tiles = row_side.shape[0]
    half = tiles // 2

    @pl.when(step_index == 0)
    def _():
        copies = [
            pltpu.make_async_copy(row_near, row_side.at[pl.ds(0, half)], sems.at[0]),
            pltpu.make_async_copy(row_far, row_side.at[pl.ds(half, half)], sems.at[1]),
            pltpu.make_async_copy(col_near, col_side.at[pl.ds(0, half)], sems.at[2]),
            pltpu.make_async_copy(col_far, col_side.at[pl.ds(half, half)], sems.at[3]),
        ]
        for c in copies:
            c.start()
        row_acc[...] = jnp.zeros_like(row_acc)
        col_acc[...] = jnp.zeros_like(col_acc)
        for c in copies:
            c.wait()

    def run(blocks_ref, part):
        first = (step_index - part * groups) * size
        base = part * groups * size + first
        live = jnp.clip(count_ref[part] - first, 0, size)

        def body(i, carry):
            for u in range(UNROLL):
                k = i * UNROLL + u
                row = row_tile_ref[base + k]
                col = col_tile_ref[base + k]
                block = blocks_ref[k]
                row_acc[row] += jnp.dot(
                    block, col_side[col & (tiles - 1)], preferred_element_type=jnp.float32
                )
                col_acc[col] += lax.dot_general(
                    block, row_side[row & (tiles - 1)], (((0,), (0,)), ((), ())),
                    preferred_element_type=jnp.float32,
                )
            return carry

        lax.fori_loop(0, (live + UNROLL - 1) // UNROLL, body, 0)

    @pl.when(step_index < groups)
    def _():
        run(own_ref, 0)

    @pl.when(step_index >= groups)
    def _():
        run(mate_ref, 1)

    @pl.when(step_index == 2 * groups - 1)
    def _():
        row_send[...] = row_acc[half:tiles].astype(row_send.dtype)
        row_keep[...] = row_acc[:half]
        col_send[...] = col_acc[half:tiles].astype(col_send.dtype)
        col_keep[...] = col_acc[:half]


def slot_products(row_tiles, col_tiles, counts, own, mate, row_parts, col_parts):
    slots, order, _ = own.shape
    half, _, width = row_parts[0].shape
    tiles = 2 * half
    groups = slots // GROUP

    def last(count, part):
        return jnp.maximum((count[part] + GROUP - 1) // GROUP - 1, 0)

    def own_map(g, rows, cols, count):
        return (jnp.minimum(g, last(count, 0)), 0, 0)

    def mate_map(g, rows, cols, count):
        return (jnp.clip(g - groups, 0, last(count, 1)), 0, 0)

    def whole(g, rows, cols, count):
        return (0, 0, 0)

    part = (half, order, width)
    return pl.pallas_call(
        slot_kernel,
        grid_spec=pltpu.PrefetchScalarGridSpec(
            num_scalar_prefetch=3,
            grid=(2 * groups,),
            in_specs=[
                pl.BlockSpec((GROUP, order, order), own_map),
                pl.BlockSpec((GROUP, order, order), mate_map),
            ]
            + [pl.BlockSpec(memory_space=pl.ANY)] * 4,
            out_specs=[pl.BlockSpec(part, whole, pipeline_mode=pl.Buffered(1))] * 4,
            scratch_shapes=[
                pltpu.VMEM((tiles, order, width), jnp.bfloat16),
                pltpu.VMEM((tiles, order, width), jnp.bfloat16),
                pltpu.VMEM((tiles + 1, order, width), jnp.float32),
                pltpu.VMEM((tiles + 1, order, width), jnp.float32),
                pltpu.SemaphoreType.DMA((4,)),
            ],
        ),
        out_shape=[
            jax.ShapeDtypeStruct(part, jnp.bfloat16),
            jax.ShapeDtypeStruct(part, jnp.float32),
        ]
        * 2,
        compiler_params=pltpu.CompilerParams(vmem_limit_bytes=40 * 1024 * 1024),
        cost_estimate=pl.CostEstimate(
            flops=8 * slots * order * order * width, bytes_accessed=26 * 1024 * 1024, transcendentals=0
        ),
    )(row_tiles, col_tiles, counts, own, mate, *row_parts, *col_parts)


def gather(operand, moves):
    near = jnp.concatenate([operand, move(operand, moves[0])])
    near = jnp.concatenate([near, move(near, moves[1])])
    return near, move(near, moves[2])


def scatter_sum(send, keep, moves):
    for m in (moves[2], moves[1]):
        total = keep + move(send, m).astype(jnp.float32)
        half = total.shape[0] // 2
        keep, send = total[:half], total[half:].astype(jnp.bfloat16)
    return keep + move(send, moves[0]).astype(jnp.float32)


def place_of(near_bit, ring, core):
    high, low = ring >> 1, ring & 1
    mixed = high ^ low
    third = jnp.where(core == 0, high, mixed)
    second = jnp.where(core == 0, mixed, high)
    return third * 4 + second * 2 + near_bit


def per_device(vectors, blocks, block_rows, block_cols, block_count, lower_edge, upper_edge):
    center = (upper_edge[0] + lower_edge[0]) * 0.5
    half_width = (upper_edge[0] - lower_edge[0]) * 0.5
    own = blocks[0, 0]
    slots, order, _ = own.shape
    seg, width = vectors.shape
    half = width // 2
    row_at, col_at = lax.axis_index("row"), lax.axis_index("col")
    core = col_at & 1

    mine = jnp.where(core == 0, vectors[:, :half], vectors[:, half:])
    other = move(jnp.where(core == 0, vectors[:, half:], vectors[:, :half]), TO_CORE)
    operand = jnp.where(
        core == 0, jnp.concatenate([mine, other]), jnp.concatenate([other, mine])
    )
    table = jnp.concatenate(
        [block_rows[0, 0], block_cols[0, 0], jnp.broadcast_to(block_count[0, 0], (order,))]
    )
    mate_table = move(table, TO_CORE)
    mate = move(own, TO_CORE)

    def tiles_of(table, source_core):
        rows, cols, count = table[:slots], table[slots : 2 * slots], table[2 * slots]
        live = jnp.arange(slots) < count
        place = place_of((rows >> 5) ^ (col_at >> 3), ((rows >> 3) & 3) ^ ((col_at >> 1) & 3), core)
        row_tiles = place * 8 + (rows & 7)
        place = place_of((cols >> 4) ^ (row_at >> 2), ((cols >> 2) & 3) ^ (row_at & 3), core)
        col_tiles = place * 8 + source_core * 4 + (cols & 3)
        return jnp.where(live, row_tiles, 64), jnp.where(live, col_tiles, 64), count

    own_rows, own_cols, own_count = tiles_of(table, core)
    mate_rows, mate_cols, mate_count = tiles_of(mate_table, 1 - core)
    row_tiles = jnp.concatenate([own_rows, mate_rows])
    col_tiles = jnp.concatenate([own_cols, mate_cols])
    counts = jnp.stack([own_count, mate_count])

    current = operand.astype(jnp.float32)
    previous = jnp.zeros_like(current)
    for degree in range(DEGREE):
        tiled = current.astype(jnp.bfloat16).reshape(-1, order, half)
        col_parts = gather(tiled, COL_MOVES)
        row_parts = gather(tiled, ROW_MOVES)
        row_send, row_keep, col_send, col_keep = slot_products(
            row_tiles, col_tiles, counts, own, mate, row_parts, col_parts
        )
        applied = scatter_sum(row_send, row_keep, ROW_MOVES) + scatter_sum(
            col_send, col_keep, COL_MOVES
        )
        shifted = applied.reshape(2 * seg, half) - center * current
        if degree == 0:
            following = shifted / half_width
        else:
            following = 2.0 * shifted / half_width - previous
        previous, current = (current, following)

    mine = jnp.where(core == 0, current[:seg], current[seg:])
    other = move(jnp.where(core == 0, current[seg:], current[:seg]), TO_CORE)
    return jnp.where(
        core == 0, jnp.concatenate([mine, other], 1), jnp.concatenate([other, mine], 1)
    )


def solution(mesh):
    return jax.shard_map(
        per_device,
        mesh=mesh,
        in_specs=(
            P(("row", "col"), None),
            P("row", "col", None, None, None),
            P("row", "col", None),
            P("row", "col", None),
            P("row", "col"),
            P(),
            P(),
        ),
        out_specs=P(("row", "col"), None),
        check_vma=False,
    )
```

```python
import functools
import itertools

import jax
import jax.numpy as jnp
from jax import lax
from jax.experimental import pallas as pl
from jax.experimental.pallas import tpu as pltpu
from jax.sharding import PartitionSpec as P

DEGREE = 2
UNROLL = 16
GROUP = 64
BOTH = ("row", "col")


def linear(y_hi, z, y_lo, x, core):
    return (y_hi * 4 + z) * 16 + y_lo * 8 + x * 2 + core


def pairs(move):
    every = itertools.product(range(2), range(4), range(2), range(4), range(2))
    return [(linear(*d), linear(*move(*d))) for d in every]


def ring_first(core):
    return 3 if core else 1


def ring_second(core):
    return 1 if core else 3


TO_CORE = pairs(lambda h, z, l, x, k: (h, z, l, x, k ^ 1))
ROW_MOVES = (
    pairs(lambda h, z, l, x, k: (h, z, l ^ 1, x, k)),
    pairs(lambda h, z, l, x, k: (h, z, l, x ^ ring_first(k), k)),
    pairs(lambda h, z, l, x, k: (h, z, l, x ^ ring_second(k), k)),
)
COL_MOVES = (
    pairs(lambda h, z, l, x, k: (h ^ 1, z, l, x, k)),
    pairs(lambda h, z, l, x, k: (h, z ^ ring_first(k), l, x, k)),
    pairs(lambda h, z, l, x, k: (h, z ^ ring_second(k), l, x, k)),
)


def move(value, table):
    return lax.ppermute(value, BOTH, table)


def slot_kernel(row_tile_ref, col_tile_ref, count_ref, own_ref, mate_ref, *rest):
    row_parts, col_parts, outs = rest[:4], rest[4:8], rest[8:16]
    blocks, row_side, col_side, row_acc, col_acc, cast, side_sems, block_sems, out_sems = rest[16:]
    slots = own_ref.shape[0]
    groups = slots // GROUP
    tiles = row_side.shape[0]
    quarter = tiles // 4

    def live_of(group):
        count = count_ref[group // groups]
        return jnp.clip(count - (group % groups) * GROUP, 0, GROUP)

    def block_copy(group):
        source = own_ref if group < groups else mate_ref
        return pltpu.make_async_copy(
            source.at[pl.ds((group % groups) * GROUP, GROUP)],
            blocks.at[pl.ds(group * GROUP, GROUP)],
            block_sems.at[group],
        )

    def start_if_live(group):
        @pl.when(live_of(group) > 0)
        def _():
            block_copy(group).start()

    copies = []
    for side, parts in ((col_side, col_parts), (row_side, row_parts)):
        for i, part in enumerate(parts):
            copies.append(
                pltpu.make_async_copy(
                    part, side.at[pl.ds(i * quarter, quarter)], side_sems.at[len(copies)]
                )
            )
    start_if_live(0)
    for c in copies:
        c.start()
    row_acc[...] = jnp.zeros_like(row_acc)
    for group in range(1, 2 * groups):
        start_if_live(group)
    col_acc[...] = jnp.zeros_like(col_acc)
    for c in copies:
        c.wait()

    def one_group(group, carry):
        live = live_of(group)

        @pl.when(live > 0)
        def _():
            pltpu.make_async_copy(
                own_ref.at[pl.ds(0, GROUP)],
                blocks.at[pl.ds(group * GROUP, GROUP)],
                block_sems.at[group],
            ).wait()

        def body(i, inner):
            for u in range(UNROLL):
                k = group * GROUP + i * UNROLL + u
                row = row_tile_ref[k]
                col = col_tile_ref[k]
                block = blocks[k]
                row_acc[row] += jnp.dot(
                    block, col_side[col & (tiles - 1)], preferred_element_type=jnp.float32
                )
                col_acc[col] += lax.dot_general(
                    block, row_side[row & (tiles - 1)], (((0,), (0,)), ((), ())),
                    preferred_element_type=jnp.float32,
                )
            return inner

        return lax.fori_loop(0, (live + UNROLL - 1) // UNROLL, body, carry)

    lax.fori_loop(0, 2 * groups, one_group, 0)

    finals = []

    def hand_out(source, out):
        copy = pltpu.make_async_copy(source, out, out_sems.at[len(finals)])
        copy.start()
        finals.append(copy)

    for acc, base in ((row_acc, 0), (col_acc, 4)):
        for i, at in enumerate((2, 0)):
            hand_out(acc.at[pl.ds(at * quarter, quarter)], outs[base + 2 + i])
    for j, (acc, base) in enumerate(((row_acc, 0), (col_acc, 4))):
        for i, at in enumerate((3, 1)):
            cast[2 * j + i] = acc[at * quarter : (at + 1) * quarter].astype(cast.dtype)
            hand_out(cast.at[2 * j + i], outs[base + i])
    for c in finals:
        c.wait()


def slot_products(row_tiles, col_tiles, counts, own, mate, row_parts, col_parts):
    slots, order, _ = own.shape
    quarter, _, width = row_parts[0].shape
    tiles = 4 * quarter
    anywhere = pl.BlockSpec(memory_space=pl.ANY)
    in_smem = pl.BlockSpec(memory_space=pltpu.SMEM)
    sent = jax.ShapeDtypeStruct((quarter, order, width), jnp.bfloat16)
    kept = jax.ShapeDtypeStruct((quarter, order, width), jnp.float32)
    return pl.pallas_call(
        slot_kernel,
        in_specs=[in_smem] * 3 + [anywhere] * 10,
        out_specs=[anywhere] * 8,
        out_shape=[sent, sent, kept, kept] * 2,
        scratch_shapes=[
            pltpu.VMEM((2 * slots, order, order), jnp.bfloat16),
            pltpu.VMEM((tiles, order, width), jnp.bfloat16),
            pltpu.VMEM((tiles, order, width), jnp.bfloat16),
            pltpu.VMEM((tiles + 1, order, width), jnp.float32),
            pltpu.VMEM((tiles + 1, order, width), jnp.float32),
            pltpu.VMEM((4, quarter, order, width), jnp.bfloat16),
            pltpu.SemaphoreType.DMA((8,)),
            pltpu.SemaphoreType.DMA((2 * slots // GROUP,)),
            pltpu.SemaphoreType.DMA((8,)),
        ],
        compiler_params=pltpu.CompilerParams(vmem_limit_bytes=36 * 1024 * 1024),
        cost_estimate=pl.CostEstimate(
            flops=8 * slots * order * order * width, bytes_accessed=26 * 1024 * 1024, transcendentals=0
        ),
    )(row_tiles, col_tiles, counts, own, mate, *row_parts, *col_parts)


def gather(operand, moves):
    across, first, second = moves
    parts = []
    for value in (operand, move(operand, across)):
        near = jnp.concatenate([value, move(value, first)])
        parts += [near, move(near, second)]
    return parts


def scatter_sum(sent_first, sent_next, kept_first, kept_next, moves):
    across, first, second = moves
    half = kept_first.shape[0] // 2
    sums = []
    for keep, send in ((kept_first, sent_first), (kept_next, sent_next)):
        near = keep + move(send, second).astype(jnp.float32)
        sums.append(
            near[:half] + move(near[half:].astype(jnp.bfloat16), first).astype(jnp.float32)
        )
    return sums[1] + move(sums[0].astype(jnp.bfloat16), across).astype(jnp.float32)


def place_of(near_bit, ring, core):
    high, low = ring >> 1, ring & 1
    mixed = high ^ low
    third = jnp.where(core == 0, high, mixed)
    second = jnp.where(core == 0, mixed, high)
    return near_bit * 4 + third * 2 + second


def per_device(vectors, blocks, block_rows, block_cols, block_count, lower_edge, upper_edge):
    center = (upper_edge[0] + lower_edge[0]) * 0.5
    half_width = (upper_edge[0] - lower_edge[0]) * 0.5
    own = blocks[0, 0]
    slots, order, _ = own.shape
    seg, width = vectors.shape
    half = width // 2
    row_at, col_at = lax.axis_index("row"), lax.axis_index("col")
    core = col_at & 1

    mine = jnp.where(core == 0, vectors[:, :half], vectors[:, half:])
    other = move(jnp.where(core == 0, vectors[:, half:], vectors[:, :half]), TO_CORE)
    table = jnp.concatenate(
        [block_rows[0, 0], block_cols[0, 0], jnp.broadcast_to(block_count[0, 0], (order,))]
    )
    other, table, own = lax.optimization_barrier((other, table, own))
    mate_table = move(table, TO_CORE)
    mate = move(own, TO_CORE)
    operand = jnp.where(
        core == 0, jnp.concatenate([mine, other]), jnp.concatenate([other, mine])
    )

    def tiles_of(table, source_core):
        rows, cols, count = table[:slots], table[slots : 2 * slots], table[2 * slots]
        live = jnp.arange(slots) < count
        place = place_of((rows >> 5) ^ (col_at >> 3), ((rows >> 3) & 3) ^ ((col_at >> 1) & 3), core)
        row_tiles = place * 8 + (rows & 7)
        place = place_of((cols >> 4) ^ (row_at >> 2), ((cols >> 2) & 3) ^ (row_at & 3), core)
        col_tiles = place * 8 + source_core * 4 + (cols & 3)
        return jnp.where(live, row_tiles, 64), jnp.where(live, col_tiles, 64), count

    own_rows, own_cols, own_count = tiles_of(table, core)
    mate_rows, mate_cols, mate_count = tiles_of(mate_table, 1 - core)
    row_tiles = jnp.concatenate([own_rows, mate_rows])
    col_tiles = jnp.concatenate([own_cols, mate_cols])
    counts = jnp.stack([own_count, mate_count])

    current = operand.astype(jnp.float32)
    previous = jnp.zeros_like(current)
    for degree in range(DEGREE):
        tiled = current.astype(jnp.bfloat16).reshape(-1, order, half)
        col_parts = gather(tiled, COL_MOVES)
        row_parts = gather(tiled, ROW_MOVES)
        found = slot_products(row_tiles, col_tiles, counts, own, mate, row_parts, col_parts)
        applied = scatter_sum(*found[:4], ROW_MOVES) + scatter_sum(*found[4:], COL_MOVES)
        shifted = applied.reshape(2 * seg, half) - center * current
        if degree == 0:
            following = shifted / half_width
        else:
            following = 2.0 * shifted / half_width - previous
        previous, current = (current, following)

    mine = jnp.where(core == 0, current[:seg], current[seg:])
    other = move(jnp.where(core == 0, current[seg:], current[:seg]), TO_CORE)
    return jnp.where(
        core == 0, jnp.concatenate([mine, other], 1), jnp.concatenate([other, mine], 1)
    )


def solution(mesh):
    return jax.shard_map(
        per_device,
        mesh=mesh,
        in_specs=(
            P(("row", "col"), None),
            P("row", "col", None, None, None),
            P("row", "col", None),
            P("row", "col", None),
            P("row", "col"),
            P(),
            P(),
        ),
        out_specs=P(("row", "col"), None),
        check_vma=False,
    )
```

```python
import functools
import itertools

import jax
import jax.numpy as jnp
from jax import lax
from jax.experimental import pallas as pl
from jax.experimental.pallas import tpu as pltpu
from jax.sharding import PartitionSpec as P

DEGREE = 2
UNROLL = 16
GROUP = 64
BOTH = ("row", "col")
ROW_FLIPS = (0, 1)
COL_FLIPS = (0, 1)


def linear(y_hi, z, y_lo, x, core):
    return (y_hi * 4 + z) * 16 + y_lo * 8 + x * 2 + core


def pairs(move):
    every = itertools.product(range(2), range(4), range(2), range(4), range(2))
    return [(linear(*d), linear(*move(*d))) for d in every]


def ring_first(core):
    return 3 if core else 1


def ring_second(core):
    return 1 if core else 3


TO_CORE = pairs(lambda h, z, l, x, k: (h, z, l, x, k ^ 1))


def row_moves(flip):
    return (
        pairs(lambda h, z, l, x, k: (h, z, l ^ 1, x, k)),
        pairs(lambda h, z, l, x, k: (h, z, l, x ^ ring_first(k ^ flip), k)),
        pairs(lambda h, z, l, x, k: (h, z, l, x ^ ring_second(k ^ flip), k)),
    )


def col_moves(flip):
    return (
        pairs(lambda h, z, l, x, k: (h ^ 1, z, l, x, k)),
        pairs(lambda h, z, l, x, k: (h, z ^ ring_first(k ^ flip), l, x, k)),
        pairs(lambda h, z, l, x, k: (h, z ^ ring_second(k ^ flip), l, x, k)),
    )


def move(value, table):
    return lax.ppermute(value, BOTH, table)


def slot_kernel(row_tile_ref, col_tile_ref, count_ref, own_ref, mate_ref, *rest):
    row_parts, col_parts, outs = rest[:4], rest[4:8], rest[8:16]
    blocks, row_side, col_side, row_acc, col_acc, cast, side_sems, block_sems, out_sems = rest[16:]
    slots = own_ref.shape[0]
    groups = slots // GROUP
    tiles = row_side.shape[0]
    quarter = tiles // 4

    def live_of(group):
        count = count_ref[group // groups]
        return jnp.clip(count - (group % groups) * GROUP, 0, GROUP)

    def block_copy(group):
        source = own_ref if group < groups else mate_ref
        return pltpu.make_async_copy(
            source.at[pl.ds((group % groups) * GROUP, GROUP)],
            blocks.at[pl.ds(group * GROUP, GROUP)],
            block_sems.at[group],
        )

    def start_if_live(group):
        @pl.when(live_of(group) > 0)
        def _():
            block_copy(group).start()

    copies = []
    for side, parts in ((col_side, col_parts), (row_side, row_parts)):
        for i, part in enumerate(parts):
            copies.append(
                pltpu.make_async_copy(
                    part, side.at[pl.ds(i * quarter, quarter)], side_sems.at[len(copies)]
                )
            )
    start_if_live(0)
    for c in copies:
        c.start()
    row_acc[...] = jnp.zeros_like(row_acc)
    for group in range(1, 2 * groups):
        start_if_live(group)
    col_acc[...] = jnp.zeros_like(col_acc)
    for c in copies:
        c.wait()

    def one_group(group, carry):
        live = live_of(group)

        @pl.when(live > 0)
        def _():
            pltpu.make_async_copy(
                own_ref.at[pl.ds(0, GROUP)],
                blocks.at[pl.ds(group * GROUP, GROUP)],
                block_sems.at[group],
            ).wait()

        def body(i, inner):
            for u in range(UNROLL):
                k = group * GROUP + i * UNROLL + u
                row = row_tile_ref[k]
                col = col_tile_ref[k]
                block = blocks[k]
                row_acc[row] += jnp.dot(
                    block, col_side[col & (tiles - 1)], preferred_element_type=jnp.float32
                )
                col_acc[col] += lax.dot_general(
                    block, row_side[row & (tiles - 1)], (((0,), (0,)), ((), ())),
                    preferred_element_type=jnp.float32,
                )
            return inner

        return lax.fori_loop(0, (live + UNROLL - 1) // UNROLL, body, carry)

    lax.fori_loop(0, 2 * groups, one_group, 0)

    finals = []

    def hand_out(source, out):
        copy = pltpu.make_async_copy(source, out, out_sems.at[len(finals)])
        copy.start()
        finals.append(copy)

    for acc, base in ((row_acc, 0), (col_acc, 4)):
        for i, at in enumerate((2, 0)):
            hand_out(acc.at[pl.ds(at * quarter, quarter)], outs[base + 2 + i])
    for j, (acc, base) in enumerate(((row_acc, 0), (col_acc, 4))):
        for i, at in enumerate((3, 1)):
            cast[2 * j + i] = acc[at * quarter : (at + 1) * quarter].astype(cast.dtype)
            hand_out(cast.at[2 * j + i], outs[base + i])
    for c in finals:
        c.wait()


def slot_products(row_tiles, col_tiles, counts, own, mate, row_parts, col_parts):
    slots, order, _ = own.shape
    quarter, _, width = row_parts[0].shape
    tiles = 4 * quarter
    anywhere = pl.BlockSpec(memory_space=pl.ANY)
    in_smem = pl.BlockSpec(memory_space=pltpu.SMEM)
    sent = jax.ShapeDtypeStruct((quarter, order, width), jnp.bfloat16)
    kept = jax.ShapeDtypeStruct((quarter, order, width), jnp.float32)
    return pl.pallas_call(
        slot_kernel,
        in_specs=[in_smem] * 3 + [anywhere] * 10,
        out_specs=[anywhere] * 8,
        out_shape=[sent, sent, kept, kept] * 2,
        scratch_shapes=[
            pltpu.VMEM((2 * slots, order, order), jnp.bfloat16),
            pltpu.VMEM((tiles, order, width), jnp.bfloat16),
            pltpu.VMEM((tiles, order, width), jnp.bfloat16),
            pltpu.VMEM((tiles + 1, order, width), jnp.float32),
            pltpu.VMEM((tiles + 1, order, width), jnp.float32),
            pltpu.VMEM((4, quarter, order, width), jnp.bfloat16),
            pltpu.SemaphoreType.DMA((8,)),
            pltpu.SemaphoreType.DMA((2 * slots // GROUP,)),
            pltpu.SemaphoreType.DMA((8,)),
        ],
        compiler_params=pltpu.CompilerParams(vmem_limit_bytes=36 * 1024 * 1024),
        cost_estimate=pl.CostEstimate(
            flops=8 * slots * order * order * width, bytes_accessed=26 * 1024 * 1024, transcendentals=0
        ),
    )(row_tiles, col_tiles, counts, own, mate, *row_parts, *col_parts)


def gather(operand, moves):
    across, first, second = moves
    parts = []
    for value in (operand, move(operand, across)):
        near = jnp.concatenate([value, move(value, first)])
        parts += [near, move(near, second)]
    return parts


def scatter_sum(sent_first, sent_next, kept_first, kept_next, moves):
    across, first, second = moves
    half = kept_first.shape[0] // 2
    got = move(sent_first, second)
    got, sent_next = lax.optimization_barrier((got, sent_next))
    near = kept_first + got.astype(jnp.float32)
    sum_first = near[:half] + move(near[half:].astype(jnp.bfloat16), first).astype(jnp.float32)
    got = move(sent_next, second)
    near = kept_next + got.astype(jnp.float32)
    sum_next = near[:half] + move(near[half:].astype(jnp.bfloat16), first).astype(jnp.float32)
    return sum_next + move(sum_first.astype(jnp.bfloat16), across).astype(jnp.float32)


def place_of(near_bit, ring, core):
    high, low = ring >> 1, ring & 1
    mixed = high ^ low
    third = jnp.where(core == 0, high, mixed)
    second = jnp.where(core == 0, mixed, high)
    return near_bit * 4 + third * 2 + second


def per_device(vectors, blocks, block_rows, block_cols, block_count, lower_edge, upper_edge):
    center = (upper_edge[0] + lower_edge[0]) * 0.5
    half_width = (upper_edge[0] - lower_edge[0]) * 0.5
    own = blocks[0, 0]
    slots, order, _ = own.shape
    seg, width = vectors.shape
    half = width // 2
    row_at, col_at = lax.axis_index("row"), lax.axis_index("col")
    core = col_at & 1

    mine = jnp.where(core == 0, vectors[:, :half], vectors[:, half:])
    other = move(jnp.where(core == 0, vectors[:, half:], vectors[:, :half]), TO_CORE)
    table = jnp.concatenate(
        [block_rows[0, 0], block_cols[0, 0], jnp.broadcast_to(block_count[0, 0], (order,))]
    )
    other, table, own = lax.optimization_barrier((other, table, own))
    mate_table = move(table, TO_CORE)
    mate = move(own, TO_CORE)
    operand = jnp.where(
        core == 0, jnp.concatenate([mine, other]), jnp.concatenate([other, mine])
    )

    def tiles_of(table, source_core, row_core, col_core):
        rows, cols, count = table[:slots], table[slots : 2 * slots], table[2 * slots]
        live = jnp.arange(slots) < count
        place = place_of(
            (rows >> 5) ^ (col_at >> 3), ((rows >> 3) & 3) ^ ((col_at >> 1) & 3), row_core
        )
        row_tiles = place * 8 + (rows & 7)
        place = place_of((cols >> 4) ^ (row_at >> 2), ((cols >> 2) & 3) ^ (row_at & 3), col_core)
        col_tiles = place * 8 + source_core * 4 + (cols & 3)
        return jnp.where(live, row_tiles, 64), jnp.where(live, col_tiles, 64)

    counts = jnp.stack([table[2 * slots], mate_table[2 * slots]])

    current = operand.astype(jnp.float32)
    previous = jnp.zeros_like(current)
    for degree in range(DEGREE):
        tiled = current.astype(jnp.bfloat16).reshape(-1, order, half)
        row_flip, col_flip = ROW_FLIPS[degree % 2], COL_FLIPS[degree % 2]
        row_plan, col_plan = row_moves(row_flip), col_moves(col_flip)
        own_tiles = tiles_of(table, core, core ^ row_flip, core ^ col_flip)
        mate_tiles = tiles_of(mate_table, 1 - core, core ^ row_flip, core ^ col_flip)
        row_tiles, col_tiles = (jnp.concatenate(pair) for pair in zip(own_tiles, mate_tiles))
        col_parts = gather(tiled, col_plan)
        row_parts = gather(tiled, row_plan)
        found = slot_products(row_tiles, col_tiles, counts, own, mate, row_parts, col_parts)
        applied = scatter_sum(*found[:4], row_plan) + scatter_sum(*found[4:], col_plan)
        shifted = applied.reshape(2 * seg, half) - center * current
        if degree == 0:
            following = shifted / half_width
        else:
            following = 2.0 * shifted / half_width - previous
        previous, current = (current, following)

    mine = jnp.where(core == 0, current[:seg], current[seg:])
    other = move(jnp.where(core == 0, current[seg:], current[:seg]), TO_CORE)
    return jnp.where(
        core == 0, jnp.concatenate([mine, other], 1), jnp.concatenate([other, mine], 1)
    )


def solution(mesh):
    return jax.shard_map(
        per_device,
        mesh=mesh,
        in_specs=(
            P(("row", "col"), None),
            P("row", "col", None, None, None),
            P("row", "col", None),
            P("row", "col", None),
            P("row", "col"),
            P(),
            P(),
        ),
        out_specs=P(("row", "col"), None),
        check_vma=False,
    )
```

```python
import functools
import itertools

import jax
import jax.numpy as jnp
from jax import lax
from jax.experimental import pallas as pl
from jax.experimental.pallas import tpu as pltpu
from jax.sharding import PartitionSpec as P

DEGREE = 2
UNROLL = 32
GROUP = 64
BOTH = ("row", "col")
ROW_FLIPS = (1, 0)
COL_FLIPS = (1, 0)


def linear(y_hi, z, y_lo, x, core):
    return (y_hi * 4 + z) * 16 + y_lo * 8 + x * 2 + core


def pairs(move):
    every = itertools.product(range(2), range(4), range(2), range(4), range(2))
    return [(linear(*d), linear(*move(*d))) for d in every]


def ring_first(core):
    return 3 if core else 1


def ring_second(core):
    return 1 if core else 3


TO_CORE = pairs(lambda h, z, l, x, k: (h, z, l, x, k ^ 1))


def row_moves(flip):
    return (
        pairs(lambda h, z, l, x, k: (h, z, l ^ 1, x, k)),
        pairs(lambda h, z, l, x, k: (h, z, l, x ^ ring_first(k ^ flip), k)),
        pairs(lambda h, z, l, x, k: (h, z, l, x ^ ring_second(k ^ flip), k)),
    )


def col_moves(flip):
    return (
        pairs(lambda h, z, l, x, k: (h ^ 1, z, l, x, k)),
        pairs(lambda h, z, l, x, k: (h, z ^ ring_first(k ^ flip), l, x, k)),
        pairs(lambda h, z, l, x, k: (h, z ^ ring_second(k ^ flip), l, x, k)),
    )


def move(value, table):
    return lax.ppermute(value, BOTH, table)


def slot_kernel(row_tile_ref, col_tile_ref, count_ref, own_ref, mate_ref, *rest):
    row_parts, col_parts, outs = rest[:4], rest[4:8], rest[8:16]
    blocks, row_side, col_side, row_acc, col_acc, cast, side_sems, block_sems, out_sems = rest[16:]
    slots = own_ref.shape[0]
    groups = slots // GROUP
    tiles = row_side.shape[0]
    quarter = tiles // 4

    def live_of(group):
        count = count_ref[group // groups]
        return jnp.clip(count - (group % groups) * GROUP, 0, GROUP)

    def block_copy(group):
        source = own_ref if group < groups else mate_ref
        return pltpu.make_async_copy(
            source.at[pl.ds((group % groups) * GROUP, GROUP)],
            blocks.at[pl.ds(group * GROUP, GROUP)],
            block_sems.at[group],
        )

    def start_if_live(group):
        @pl.when(live_of(group) > 0)
        def _():
            block_copy(group).start()

    copies = []
    for side, parts in ((col_side, col_parts), (row_side, row_parts)):
        for i, part in enumerate(parts):
            copies.append(
                pltpu.make_async_copy(
                    part, side.at[pl.ds(i * quarter, quarter)], side_sems.at[len(copies)]
                )
            )
    start_if_live(0)
    for c in copies:
        c.start()
    row_acc[...] = jnp.zeros_like(row_acc)
    for group in range(1, 2 * groups):
        start_if_live(group)
    col_acc[...] = jnp.zeros_like(col_acc)
    for c in copies:
        c.wait()

    def one_group(group, carry):
        live = live_of(group)

        @pl.when(live > 0)
        def _():
            pltpu.make_async_copy(
                own_ref.at[pl.ds(0, GROUP)],
                blocks.at[pl.ds(group * GROUP, GROUP)],
                block_sems.at[group],
            ).wait()

        def body(i, inner):
            for u in range(UNROLL):
                k = group * GROUP + i * UNROLL + u
                row = row_tile_ref[k]
                col = col_tile_ref[k]
                block = blocks[k]
                row_acc[row] += jnp.dot(
                    block, col_side[col & (tiles - 1)], preferred_element_type=jnp.float32
                )
                col_acc[col] += lax.dot_general(
                    block, row_side[row & (tiles - 1)], (((0,), (0,)), ((), ())),
                    preferred_element_type=jnp.float32,
                )
            return inner

        return lax.fori_loop(0, (live + UNROLL - 1) // UNROLL, body, carry)

    lax.fori_loop(0, 2 * groups, one_group, 0)

    finals = []

    def hand_out(source, out):
        copy = pltpu.make_async_copy(source, out, out_sems.at[len(finals)])
        copy.start()
        finals.append(copy)

    for acc, base in ((row_acc, 0), (col_acc, 4)):
        for i, at in enumerate((2, 0)):
            hand_out(acc.at[pl.ds(at * quarter, quarter)], outs[base + 2 + i])
    for j, (acc, base) in enumerate(((row_acc, 0), (col_acc, 4))):
        for i, at in enumerate((3, 1)):
            cast[2 * j + i] = acc[at * quarter : (at + 1) * quarter].astype(cast.dtype)
            hand_out(cast.at[2 * j + i], outs[base + i])
    for c in finals:
        c.wait()


def slot_products(row_tiles, col_tiles, counts, own, mate, row_parts, col_parts):
    slots, order, _ = own.shape
    quarter, _, width = row_parts[0].shape
    tiles = 4 * quarter
    anywhere = pl.BlockSpec(memory_space=pl.ANY)
    in_smem = pl.BlockSpec(memory_space=pltpu.SMEM)
    sent = jax.ShapeDtypeStruct((quarter, order, width), jnp.bfloat16)
    kept = jax.ShapeDtypeStruct((quarter, order, width), jnp.float32)
    return pl.pallas_call(
        slot_kernel,
        in_specs=[in_smem] * 3 + [anywhere] * 10,
        out_specs=[anywhere] * 8,
        out_shape=[sent, sent, kept, kept] * 2,
        scratch_shapes=[
            pltpu.VMEM((2 * slots, order, order), jnp.bfloat16),
            pltpu.VMEM((tiles, order, width), jnp.bfloat16),
            pltpu.VMEM((tiles, order, width), jnp.bfloat16),
            pltpu.VMEM((tiles + 1, order, width), jnp.float32),
            pltpu.VMEM((tiles + 1, order, width), jnp.float32),
            pltpu.VMEM((4, quarter, order, width), jnp.bfloat16),
            pltpu.SemaphoreType.DMA((8,)),
            pltpu.SemaphoreType.DMA((2 * slots // GROUP,)),
            pltpu.SemaphoreType.DMA((8,)),
        ],
        compiler_params=pltpu.CompilerParams(vmem_limit_bytes=36 * 1024 * 1024),
        cost_estimate=pl.CostEstimate(
            flops=8 * slots * order * order * width, bytes_accessed=26 * 1024 * 1024, transcendentals=0
        ),
    )(row_tiles, col_tiles, counts, own, mate, *row_parts, *col_parts)


def gather(operand, moves):
    across, first, second = moves
    parts = []
    for value in (operand, move(operand, across)):
        near = jnp.concatenate([value, move(value, first)])
        parts += [near, move(near, second)]
    return parts


def scatter_sum(sent_first, sent_next, kept_first, kept_next, moves):
    across, first, second = moves
    half = kept_first.shape[0] // 2
    got = move(sent_first, second)
    got, sent_next = lax.optimization_barrier((got, sent_next))
    near = kept_first + got.astype(jnp.float32)
    sum_first = near[:half] + move(near[half:].astype(jnp.bfloat16), first).astype(jnp.float32)
    got = move(sent_next, second)
    near = kept_next + got.astype(jnp.float32)
    sum_next = near[:half] + move(near[half:].astype(jnp.bfloat16), first).astype(jnp.float32)
    return sum_next + move(sum_first.astype(jnp.bfloat16), across).astype(jnp.float32)


def place_of(near_bit, ring, core):
    high, low = ring >> 1, ring & 1
    mixed = high ^ low
    third = jnp.where(core == 0, high, mixed)
    second = jnp.where(core == 0, mixed, high)
    return near_bit * 4 + third * 2 + second


def per_device(vectors, blocks, block_rows, block_cols, block_count, lower_edge, upper_edge):
    center = (upper_edge[0] + lower_edge[0]) * 0.5
    half_width = (upper_edge[0] - lower_edge[0]) * 0.5
    own = blocks[0, 0]
    slots, order, _ = own.shape
    seg, width = vectors.shape
    half = width // 2
    row_at, col_at = lax.axis_index("row"), lax.axis_index("col")
    core = col_at & 1

    mine = jnp.where(core == 0, vectors[:, :half], vectors[:, half:])
    other = move(jnp.where(core == 0, vectors[:, half:], vectors[:, :half]), TO_CORE)
    table = jnp.concatenate(
        [block_rows[0, 0], block_cols[0, 0], jnp.broadcast_to(block_count[0, 0], (order,))]
    )
    other, table, own = lax.optimization_barrier((other, table, own))
    mate_table = move(table, TO_CORE)
    mate = move(own, TO_CORE)
    operand = jnp.where(
        core == 0, jnp.concatenate([mine, other]), jnp.concatenate([other, mine])
    )

    def tiles_of(table, source_core, row_core, col_core):
        rows, cols, count = table[:slots], table[slots : 2 * slots], table[2 * slots]
        live = jnp.arange(slots) < count
        place = place_of(
            (rows >> 5) ^ (col_at >> 3), ((rows >> 3) & 3) ^ ((col_at >> 1) & 3), row_core
        )
        row_tiles = place * 8 + (rows & 7)
        place = place_of((cols >> 4) ^ (row_at >> 2), ((cols >> 2) & 3) ^ (row_at & 3), col_core)
        col_tiles = place * 8 + source_core * 4 + (cols & 3)
        return jnp.where(live, row_tiles, 64), jnp.where(live, col_tiles, 64)

    counts = jnp.stack([table[2 * slots], mate_table[2 * slots]])

    current = operand.astype(jnp.float32)
    previous = jnp.zeros_like(current)
    for degree in range(DEGREE):
        tiled = current.astype(jnp.bfloat16).reshape(-1, order, half)
        row_flip, col_flip = ROW_FLIPS[degree % 2], COL_FLIPS[degree % 2]
        row_plan, col_plan = row_moves(row_flip), col_moves(col_flip)
        own_tiles = tiles_of(table, core, core ^ row_flip, core ^ col_flip)
        mate_tiles = tiles_of(mate_table, 1 - core, core ^ row_flip, core ^ col_flip)
        row_tiles, col_tiles = (jnp.concatenate(pair) for pair in zip(own_tiles, mate_tiles))
        col_parts = gather(tiled, col_plan)
        row_parts = gather(tiled, row_plan)
        found = slot_products(row_tiles, col_tiles, counts, own, mate, row_parts, col_parts)
        applied = scatter_sum(*found[:4], row_plan) + scatter_sum(*found[4:], col_plan)
        shifted = applied.reshape(2 * seg, half) - center * current
        if degree == 0:
            following = shifted / half_width
        else:
            following = 2.0 * shifted / half_width - previous
        previous, current = (current, following)

    mine = jnp.where(core == 0, current[:seg], current[seg:])
    other = move(jnp.where(core == 0, current[seg:], current[:seg]), TO_CORE)
    return jnp.where(
        core == 0, jnp.concatenate([mine, other], 1), jnp.concatenate([other, mine], 1)
    )


def solution(mesh):
    return jax.shard_map(
        per_device,
        mesh=mesh,
        in_specs=(
            P(("row", "col"), None),
            P("row", "col", None, None, None),
            P("row", "col", None),
            P("row", "col", None),
            P("row", "col"),
            P(),
            P(),
        ),
        out_specs=P(("row", "col"), None),
        check_vma=False,
    )
```

```python
import functools
import itertools

import jax
import jax.numpy as jnp
from jax import lax
from jax.experimental import pallas as pl
from jax.experimental.pallas import tpu as pltpu
from jax.sharding import PartitionSpec as P

DEGREE = 2
UNROLL = 32
GROUP = 64
BOTH = ("row", "col")
ROW_FLIPS = (1, 0)
COL_FLIPS = (1, 0)


def linear(y_hi, z, y_lo, x, core):
    return (y_hi * 4 + z) * 16 + y_lo * 8 + x * 2 + core


def pairs(move):
    every = itertools.product(range(2), range(4), range(2), range(4), range(2))
    return [(linear(*d), linear(*move(*d))) for d in every]


def ring_first(core):
    return 3 if core else 1


def ring_second(core):
    return 1 if core else 3


TO_CORE = pairs(lambda h, z, l, x, k: (h, z, l, x, k ^ 1))


def row_moves(flip):
    return (
        pairs(lambda h, z, l, x, k: (h, z, l ^ 1, x, k)),
        pairs(lambda h, z, l, x, k: (h, z, l, x ^ ring_first(k ^ flip), k)),
        pairs(lambda h, z, l, x, k: (h, z, l, x ^ ring_second(k ^ flip), k)),
    )


def col_moves(flip):
    return (
        pairs(lambda h, z, l, x, k: (h ^ 1, z, l, x, k)),
        pairs(lambda h, z, l, x, k: (h, z ^ ring_first(k ^ flip), l, x, k)),
        pairs(lambda h, z, l, x, k: (h, z ^ ring_second(k ^ flip), l, x, k)),
    )


def move(value, table):
    return lax.ppermute(value, BOTH, table)


def slot_kernel(row_tile_ref, col_tile_ref, count_ref, own_ref, mate_ref, *rest):
    row_parts, col_parts, outs = rest[:4], rest[4:8], rest[8:16]
    blocks, row_side, col_side, row_acc, col_acc, cast, side_sems, block_sems, out_sems = rest[16:]
    slots = own_ref.shape[0]
    groups = slots // GROUP
    tiles = row_side.shape[0]
    quarter = tiles // 4

    def live_of(group):
        count = count_ref[group // groups]
        return jnp.clip(count - (group % groups) * GROUP, 0, GROUP)

    def block_copy(group):
        source = own_ref if group < groups else mate_ref
        return pltpu.make_async_copy(
            source.at[pl.ds((group % groups) * GROUP, GROUP)],
            blocks.at[pl.ds(group * GROUP, GROUP)],
            block_sems.at[group],
        )

    def start_if_live(group):
        @pl.when(live_of(group) > 0)
        def _():
            block_copy(group).start()

    copies = []
    for side, parts in ((col_side, col_parts), (row_side, row_parts)):
        for i, part in enumerate(parts):
            copies.append(
                pltpu.make_async_copy(
                    part, side.at[pl.ds(i * quarter, quarter)], side_sems.at[len(copies)]
                )
            )
    start_if_live(0)
    for c in copies:
        c.start()
    row_acc[...] = jnp.zeros_like(row_acc)
    for group in range(1, 2 * groups):
        start_if_live(group)
    col_acc[...] = jnp.zeros_like(col_acc)
    for c in copies:
        c.wait()

    def one_group(group, carry):
        live = live_of(group)

        @pl.when(live > 0)
        def _():
            pltpu.make_async_copy(
                own_ref.at[pl.ds(0, GROUP)],
                blocks.at[pl.ds(group * GROUP, GROUP)],
                block_sems.at[group],
            ).wait()

        def body(i, inner):
            for u in range(UNROLL):
                k = group * GROUP + i * UNROLL + u
                row = row_tile_ref[k]
                col = col_tile_ref[k]
                block = blocks[k]
                row_acc[row] += jnp.dot(
                    block, col_side[col & (tiles - 1)], preferred_element_type=jnp.float32
                )
                col_acc[col] += lax.dot_general(
                    block, row_side[row & (tiles - 1)], (((0,), (0,)), ((), ())),
                    preferred_element_type=jnp.float32,
                )
            return inner

        return lax.fori_loop(0, (live + UNROLL - 1) // UNROLL, body, carry)

    lax.fori_loop(0, 2 * groups, one_group, 0)

    finals = []

    def hand_out(source, out):
        copy = pltpu.make_async_copy(source, out, out_sems.at[len(finals)])
        copy.start()
        finals.append(copy)

    for acc, base in ((row_acc, 0), (col_acc, 4)):
        for i, at in enumerate((2, 0)):
            hand_out(acc.at[pl.ds(at * quarter, quarter)], outs[base + 2 + i])
    for j, (acc, base) in enumerate(((row_acc, 0), (col_acc, 4))):
        for i, at in enumerate((3, 1)):
            cast[2 * j + i] = acc[at * quarter : (at + 1) * quarter].astype(cast.dtype)
            hand_out(cast.at[2 * j + i], outs[base + i])
    for c in finals:
        c.wait()


def slot_products(row_tiles, col_tiles, counts, own, mate, row_parts, col_parts):
    slots, order, _ = own.shape
    quarter, _, width = row_parts[0].shape
    tiles = 4 * quarter
    anywhere = pl.BlockSpec(memory_space=pl.ANY)
    in_smem = pl.BlockSpec(memory_space=pltpu.SMEM)
    sent = jax.ShapeDtypeStruct((quarter, order, width), jnp.bfloat16)
    kept = jax.ShapeDtypeStruct((quarter, order, width), jnp.float32)
    return pl.pallas_call(
        slot_kernel,
        in_specs=[in_smem] * 3 + [anywhere] * 10,
        out_specs=[anywhere] * 8,
        out_shape=[sent, sent, kept, kept] * 2,
        scratch_shapes=[
            pltpu.VMEM((2 * slots, order, order), jnp.bfloat16),
            pltpu.VMEM((tiles, order, width), jnp.bfloat16),
            pltpu.VMEM((tiles, order, width), jnp.bfloat16),
            pltpu.VMEM((tiles + 1, order, width), jnp.float32),
            pltpu.VMEM((tiles + 1, order, width), jnp.float32),
            pltpu.VMEM((4, quarter, order, width), jnp.bfloat16),
            pltpu.SemaphoreType.DMA((8,)),
            pltpu.SemaphoreType.DMA((2 * slots // GROUP,)),
            pltpu.SemaphoreType.DMA((8,)),
        ],
        compiler_params=pltpu.CompilerParams(vmem_limit_bytes=36 * 1024 * 1024),
        cost_estimate=pl.CostEstimate(
            flops=8 * slots * order * order * width, bytes_accessed=26 * 1024 * 1024, transcendentals=0
        ),
    )(row_tiles, col_tiles, counts, own, mate, *row_parts, *col_parts)


def gather(operand, plans):
    mates = [move(operand, plan[0]) for plan in plans]
    nexts = [move(operand, plan[1]) for plan in plans]
    sides = []
    seconds = [move(mate, plan[1]) for plan, mate in zip(plans, mates)]
    for plan, near, mate, second in zip(plans, nexts, mates, seconds):
        own = jnp.concatenate([operand, near])
        far = jnp.concatenate([mate, second])
        sides.append([own, move(own, plan[2]), far, move(far, plan[2])])
    return sides


def halves(kept, got):
    half = kept.shape[0] // 2
    stay = kept[:half] + got[:half].astype(jnp.float32)
    return stay, (kept[half:] + got[half:].astype(jnp.float32)).astype(jnp.bfloat16)


def scatter_sum(sent_first, sent_next, kept_first, kept_next, moves):
    across, first, second = moves
    got = move(sent_first, second)
    got, sent_next = lax.optimization_barrier((got, sent_next))
    stay, send = halves(kept_first, got)
    sum_first = (stay + move(send, first).astype(jnp.float32)).astype(jnp.bfloat16)
    stay, send = halves(kept_next, move(sent_next, second))
    last = move(send, first).astype(jnp.float32)
    return (stay + move(sum_first, across).astype(jnp.float32)) + last


def place_of(near_bit, ring, core):
    high, low = ring >> 1, ring & 1
    mixed = high ^ low
    third = jnp.where(core == 0, high, mixed)
    second = jnp.where(core == 0, mixed, high)
    return near_bit * 4 + third * 2 + second


def per_device(vectors, blocks, block_rows, block_cols, block_count, lower_edge, upper_edge):
    center = (upper_edge[0] + lower_edge[0]) * 0.5
    half_width = (upper_edge[0] - lower_edge[0]) * 0.5
    own = blocks[0, 0]
    slots, order, _ = own.shape
    seg, width = vectors.shape
    half = width // 2
    row_at, col_at = lax.axis_index("row"), lax.axis_index("col")
    core = col_at & 1

    mine = jnp.where(core == 0, vectors[:, :half], vectors[:, half:])
    other = move(jnp.where(core == 0, vectors[:, half:], vectors[:, :half]), TO_CORE)
    table = jnp.concatenate(
        [block_rows[0, 0], block_cols[0, 0], jnp.broadcast_to(block_count[0, 0], (order,))]
    )
    other, table, own = lax.optimization_barrier((other, table, own))
    mate_table = move(table, TO_CORE)
    mate = move(own, TO_CORE)
    operand = jnp.where(
        core == 0, jnp.concatenate([mine, other]), jnp.concatenate([other, mine])
    )

    def tiles_of(table, source_core, row_core, col_core):
        rows, cols, count = table[:slots], table[slots : 2 * slots], table[2 * slots]
        live = jnp.arange(slots) < count
        place = place_of(
            (rows >> 5) ^ (col_at >> 3), ((rows >> 3) & 3) ^ ((col_at >> 1) & 3), row_core
        )
        row_tiles = place * 8 + (rows & 7)
        place = place_of((cols >> 4) ^ (row_at >> 2), ((cols >> 2) & 3) ^ (row_at & 3), col_core)
        col_tiles = place * 8 + source_core * 4 + (cols & 3)
        return jnp.where(live, row_tiles, 64), jnp.where(live, col_tiles, 64)

    counts = jnp.stack([table[2 * slots], mate_table[2 * slots]])

    current = operand.astype(jnp.float32)
    previous = jnp.zeros_like(current)
    for degree in range(DEGREE):
        tiled = current.astype(jnp.bfloat16).reshape(-1, order, half)
        row_flip, col_flip = ROW_FLIPS[degree % 2], COL_FLIPS[degree % 2]
        row_plan, col_plan = row_moves(row_flip), col_moves(col_flip)
        own_tiles = tiles_of(table, core, core ^ row_flip, core ^ col_flip)
        mate_tiles = tiles_of(mate_table, 1 - core, core ^ row_flip, core ^ col_flip)
        row_tiles, col_tiles = (jnp.concatenate(pair) for pair in zip(own_tiles, mate_tiles))
        col_parts, row_parts = gather(tiled, (col_plan, row_plan))
        found = slot_products(row_tiles, col_tiles, counts, own, mate, row_parts, col_parts)
        applied = scatter_sum(*found[:4], row_plan) + scatter_sum(*found[4:], col_plan)
        shifted = applied.reshape(2 * seg, half) - center * current
        if degree == 0:
            following = shifted / half_width
        else:
            following = 2.0 * shifted / half_width - previous
        previous, current = (current, following)

    mine = jnp.where(core == 0, current[:seg], current[seg:])
    other = move(jnp.where(core == 0, current[seg:], current[:seg]), TO_CORE)
    return jnp.where(
        core == 0, jnp.concatenate([mine, other], 1), jnp.concatenate([other, mine], 1)
    )


def solution(mesh):
    return jax.shard_map(
        per_device,
        mesh=mesh,
        in_specs=(
            P(("row", "col"), None),
            P("row", "col", None, None, None),
            P("row", "col", None),
            P("row", "col", None),
            P("row", "col"),
            P(),
            P(),
        ),
        out_specs=P(("row", "col"), None),
        check_vma=False,
    )
```

```python
import functools
import itertools

import jax
import jax.numpy as jnp
from jax import lax
from jax.experimental import pallas as pl
from jax.experimental.pallas import tpu as pltpu
from jax.sharding import PartitionSpec as P

DEGREE = 2
UNROLL = 32
GROUP = 64
BOTH = ("row", "col")
ROW_FLIPS = (1, 0)
COL_FLIPS = (1, 0)


def linear(y_hi, z, y_lo, x, core):
    return (y_hi * 4 + z) * 16 + y_lo * 8 + x * 2 + core


def pairs(move):
    every = itertools.product(range(2), range(4), range(2), range(4), range(2))
    return [(linear(*d), linear(*move(*d))) for d in every]


def ring_first(core):
    return 3 if core else 1


def ring_second(core):
    return 1 if core else 3


TO_CORE = pairs(lambda h, z, l, x, k: (h, z, l, x, k ^ 1))


def row_moves(flip):
    return (
        pairs(lambda h, z, l, x, k: (h, z, l ^ 1, x, k)),
        pairs(lambda h, z, l, x, k: (h, z, l, x ^ ring_first(k ^ flip), k)),
        pairs(lambda h, z, l, x, k: (h, z, l, x ^ ring_second(k ^ flip), k)),
    )


def col_moves(flip):
    return (
        pairs(lambda h, z, l, x, k: (h ^ 1, z, l, x, k)),
        pairs(lambda h, z, l, x, k: (h, z ^ ring_first(k ^ flip), l, x, k)),
        pairs(lambda h, z, l, x, k: (h, z ^ ring_second(k ^ flip), l, x, k)),
    )


def move(value, table):
    return lax.ppermute(value, BOTH, table)


def slot_kernel(row_tile_ref, col_tile_ref, count_ref, own_ref, mate_ref, *rest):
    row_parts, col_parts, outs = rest[:4], rest[4:8], rest[8:16]
    blocks, row_side, col_side, row_acc, col_acc, cast, side_sems, block_sems, out_sems = rest[16:]
    slots = own_ref.shape[0]
    groups = slots // GROUP
    tiles = row_side.shape[0]
    quarter = tiles // 4

    def live_of(group):
        count = count_ref[group // groups]
        return jnp.clip(count - (group % groups) * GROUP, 0, GROUP)

    def block_copy(group):
        source = own_ref if group < groups else mate_ref
        return pltpu.make_async_copy(
            source.at[pl.ds((group % groups) * GROUP, GROUP)],
            blocks.at[pl.ds(group * GROUP, GROUP)],
            block_sems.at[group],
        )

    def start_if_live(group):
        @pl.when(live_of(group) > 0)
        def _():
            block_copy(group).start()

    copies = []
    for side, parts in ((col_side, col_parts), (row_side, row_parts)):
        for i, part in enumerate(parts):
            copies.append(
                pltpu.make_async_copy(
                    part, side.at[pl.ds(i * quarter, quarter)], side_sems.at[len(copies)]
                )
            )
    start_if_live(0)
    for c in copies:
        c.start()
    row_acc[...] = jnp.zeros_like(row_acc)
    for group in range(1, 2 * groups):
        start_if_live(group)
    col_acc[...] = jnp.zeros_like(col_acc)
    for c in copies:
        c.wait()

    def one_group(group, carry):
        live = live_of(group)

        @pl.when(live > 0)
        def _():
            pltpu.make_async_copy(
                own_ref.at[pl.ds(0, GROUP)],
                blocks.at[pl.ds(group * GROUP, GROUP)],
                block_sems.at[group],
            ).wait()

        def body(i, inner):
            for u in range(UNROLL):
                k = group * GROUP + i * UNROLL + u
                row = row_tile_ref[k]
                col = col_tile_ref[k]
                block = blocks[k]
                row_acc[row] += jnp.dot(
                    block, col_side[col & (tiles - 1)], preferred_element_type=jnp.float32
                )
                col_acc[col] += lax.dot_general(
                    block, row_side[row & (tiles - 1)], (((0,), (0,)), ((), ())),
                    preferred_element_type=jnp.float32,
                )
            return inner

        return lax.fori_loop(0, (live + UNROLL - 1) // UNROLL, body, carry)

    lax.fori_loop(0, 2 * groups, one_group, 0)

    finals = []

    def hand_out(source, out):
        copy = pltpu.make_async_copy(source, out, out_sems.at[len(finals)])
        copy.start()
        finals.append(copy)

    for acc, base in ((row_acc, 0), (col_acc, 4)):
        for i, at in enumerate((2, 0)):
            hand_out(acc.at[pl.ds(at * quarter, quarter)], outs[base + 2 + i])
    for j, (acc, base) in enumerate(((row_acc, 0), (col_acc, 4))):
        for i, at in enumerate((3, 1)):
            cast[2 * j + i] = acc[at * quarter : (at + 1) * quarter].astype(cast.dtype)
            hand_out(cast.at[2 * j + i], outs[base + i])
    for c in finals:
        c.wait()


def slot_products(row_tiles, col_tiles, counts, own, mate, row_parts, col_parts):
    slots, order, _ = own.shape
    quarter, _, width = row_parts[0].shape
    tiles = 4 * quarter
    anywhere = pl.BlockSpec(memory_space=pl.ANY)
    in_smem = pl.BlockSpec(memory_space=pltpu.SMEM)
    sent = jax.ShapeDtypeStruct((quarter, order, width), jnp.bfloat16)
    kept = jax.ShapeDtypeStruct((quarter, order, width), jnp.float32)
    return pl.pallas_call(
        slot_kernel,
        in_specs=[in_smem] * 3 + [anywhere] * 10,
        out_specs=[anywhere] * 8,
        out_shape=[sent, sent, kept, kept] * 2,
        scratch_shapes=[
            pltpu.VMEM((2 * slots, order, order), jnp.bfloat16),
            pltpu.VMEM((tiles, order, width), jnp.bfloat16),
            pltpu.VMEM((tiles, order, width), jnp.bfloat16),
            pltpu.VMEM((tiles + 1, order, width), jnp.float32),
            pltpu.VMEM((tiles + 1, order, width), jnp.float32),
            pltpu.VMEM((4, quarter, order, width), jnp.bfloat16),
            pltpu.SemaphoreType.DMA((8,)),
            pltpu.SemaphoreType.DMA((2 * slots // GROUP,)),
            pltpu.SemaphoreType.DMA((8,)),
        ],
        compiler_params=pltpu.CompilerParams(vmem_limit_bytes=36 * 1024 * 1024),
        cost_estimate=pl.CostEstimate(
            flops=8 * slots * order * order * width, bytes_accessed=26 * 1024 * 1024, transcendentals=0
        ),
    )(row_tiles, col_tiles, counts, own, mate, *row_parts, *col_parts)


def gather(operand, plans):
    mates = [move(operand, plan[0]) for plan in plans]
    nexts = [move(operand, plan[1]) for plan in plans]
    sides = []
    seconds = [move(mate, plan[1]) for plan, mate in zip(plans, mates)]
    for plan, near, mate, second in zip(plans, nexts, mates, seconds):
        own = jnp.concatenate([operand, near])
        far = jnp.concatenate([mate, second])
        sides.append([own, move(own, plan[2]), far, move(far, plan[2])])
    return sides


def halves(kept, got):
    half = kept.shape[0] // 2
    stay = kept[:half] + got[:half].astype(jnp.float32)
    return stay, (kept[half:] + got[half:].astype(jnp.float32)).astype(jnp.bfloat16)


def scatter_sum(sent_first, sent_next, kept_first, kept_next, moves):
    across, first, second = moves
    got = move(sent_first, second)
    got, sent_next = lax.optimization_barrier((got, sent_next))
    stay, send = halves(kept_first, got)
    sum_first = (stay + move(send, first).astype(jnp.float32)).astype(jnp.bfloat16)
    stay, send = halves(kept_next, move(sent_next, second))
    last = move(send, first).astype(jnp.float32)
    return (stay + move(sum_first, across).astype(jnp.float32)) + last


def place_of(near_bit, ring, core):
    high, low = ring >> 1, ring & 1
    mixed = high ^ low
    third = jnp.where(core == 0, high, mixed)
    second = jnp.where(core == 0, mixed, high)
    return near_bit * 4 + third * 2 + second


def per_device(vectors, blocks, block_rows, block_cols, block_count, lower_edge, upper_edge):
    center = (upper_edge[0] + lower_edge[0]) * 0.5
    half_width = (upper_edge[0] - lower_edge[0]) * 0.5
    own = blocks[0, 0]
    slots, order, _ = own.shape
    seg, width = vectors.shape
    half = width // 2
    row_at, col_at = lax.axis_index("row"), lax.axis_index("col")
    core = col_at & 1

    mine = jnp.where(core == 0, vectors[:, :half], vectors[:, half:])
    other = move(jnp.where(core == 0, vectors[:, half:], vectors[:, :half]), TO_CORE)
    table = jnp.concatenate(
        [block_rows[0, 0], block_cols[0, 0], jnp.broadcast_to(block_count[0, 0], (order,))]
    )
    other, table, own = lax.optimization_barrier((other, table, own))
    mate_table = move(table, TO_CORE)
    mate = move(own, TO_CORE)
    operand = jnp.where(
        core == 0, jnp.concatenate([mine, other]), jnp.concatenate([other, mine])
    )

    def tiles_of(table, source_core, row_core, col_core):
        rows, cols, count = table[:slots], table[slots : 2 * slots], table[2 * slots]
        live = jnp.arange(slots) < count
        place = place_of(
            (rows >> 5) ^ (col_at >> 3), ((rows >> 3) & 3) ^ ((col_at >> 1) & 3), row_core
        )
        row_tiles = place * 8 + (rows & 7)
        place = place_of((cols >> 4) ^ (row_at >> 2), ((cols >> 2) & 3) ^ (row_at & 3), col_core)
        col_tiles = place * 8 + source_core * 4 + (cols & 3)
        return jnp.where(live, row_tiles, 64), jnp.where(live, col_tiles, 64)

    counts = jnp.stack([table[2 * slots], mate_table[2 * slots]])

    current = operand.astype(jnp.float32)
    previous = jnp.zeros_like(current)
    for degree in range(DEGREE):
        tiled = current.astype(jnp.bfloat16).reshape(-1, order, half)
        row_flip, col_flip = ROW_FLIPS[degree % 2], COL_FLIPS[degree % 2]
        row_plan, col_plan = row_moves(row_flip), col_moves(col_flip)
        own_tiles = tiles_of(table, core, core ^ row_flip, core ^ col_flip)
        mate_tiles = tiles_of(mate_table, 1 - core, core ^ row_flip, core ^ col_flip)
        row_tiles, col_tiles = (jnp.concatenate(pair) for pair in zip(own_tiles, mate_tiles))
        row_parts, col_parts = gather(tiled, (row_plan, col_plan))
        found = slot_products(row_tiles, col_tiles, counts, own, mate, row_parts, col_parts)
        applied = scatter_sum(*found[:4], row_plan) + scatter_sum(*found[4:], col_plan)
        shifted = applied.reshape(2 * seg, half) - center * current
        if degree == 0:
            following = shifted / half_width
        else:
            following = 2.0 * shifted / half_width - previous
        previous, current = (current, following)

    mine = jnp.where(core == 0, current[:seg], current[seg:])
    other = move(jnp.where(core == 0, current[seg:], current[:seg]), TO_CORE)
    return jnp.where(
        core == 0, jnp.concatenate([mine, other], 1), jnp.concatenate([other, mine], 1)
    )


def solution(mesh):
    return jax.shard_map(
        per_device,
        mesh=mesh,
        in_specs=(
            P(("row", "col"), None),
            P("row", "col", None, None, None),
            P("row", "col", None),
            P("row", "col", None),
            P("row", "col"),
            P(),
            P(),
        ),
        out_specs=P(("row", "col"), None),
        check_vma=False,
    )
```
